512 devices in a mesh: dp: 16 (over y, core), expert: 32 (over x, z).
Axes of the slice: x: 4, y: 8, z: 8, core: 2. Of those that a mesh axis runs over, the one named last changes fastest.
Arguments:
- tokens: bfloat16 [65536, 2048], P(('dp', 'expert')), may hold values from -24 to 24
- out_grad: bfloat16 [65536, 2048], P(('dp', 'expert')), may hold values from -3 to 3
- expert_ids: int32 [65536, 2], P(('dp', 'expert')), may hold values from 0 to 31, as said below
- route_probs: bfloat16 [65536, 2], P(('dp', 'expert')), may hold values from 0.099609375 to 0.8984375
- gate_weight: bfloat16 [32, 2048, 384], P('expert', 'dp'), may hold values from -0.125 to 0.125
- up_weight: bfloat16 [32, 2048, 384], P('expert', 'dp'), may hold values from -0.125 to 0.125
- down_weight: bfloat16 [32, 384, 2048], P('expert', None, 'dp'), may hold values from -0.3125 to 0.3125
- gate_mask: int32 [32, 512, 384], P('expert', 'dp'), may hold values from 0 to 5
- up_mask: int32 [32, 512, 384], P('expert', 'dp'), may hold values from 0 to 5
- down_mask: int32 [32, 96, 2048], P('expert', None, 'dp'), may hold values from 0 to 5
Outputs:
- token_grad: bfloat16 [65536, 2048], P(('dp', 'expert'))
- prob_grad: bfloat16 [65536, 2], P(('dp', 'expert'))
- gate_grad: float32 [32, 2048, 384], P('expert', 'dp')
- up_grad: float32 [32, 2048, 384], P('expert', 'dp')
The draws below stay inside these ranges and needn't reach their ends.
Inputs may be any that keep to these rules, and one draw needn't show every extreme that they name: `expert_ids`: each row names 2 different experts. The rows of one device name no expert more than 12 times; in every draw some expert is named exactly 12 times by the rows of every device of some data group.
All inputs are finite; a program needn't handle non-finite values.
Results may differ from the reference program's by a relative error of at most 0.02.
Values may be sent and summed in bfloat16 or wider, within the bound.
No kernel may reach another device: no remote copies, remote signals or barrier semaphores. Data moves between devices by JAX's collectives and lax.ppermute only.
A program may use at most 64 MiB of HBM per device.

```python
import math
import jax
import jax.numpy as jnp
import numpy as np
from jax import lax

D = 2048
HW = 384
TOPK = 2
TOK_DEV = 128
EXPERTS = 32
CAP = 12
TOKENS = 65536
N_DP = 16
N_EXPERT = 32


def draw_expert_ids(key, part):
    blocks = TOKENS // TOK_DEV
    groups = blocks // EXPERTS
    key_perm, key_rank, key_turn, key_hot, key_flag, key_force = jax.random.split(key, 6)
    perm_table = jax.vmap(lambda subkey: jax.random.permutation(subkey, EXPERTS))(jax.random.split(key_perm, blocks))
    rank_table = jax.vmap(lambda subkey: jax.random.permutation(subkey, TOK_DEV))(jax.random.split(key_rank, blocks))
    hot_group = jax.random.randint(key_hot, (groups,), 0, EXPERTS)
    flag_draw = jax.random.randint(key_flag, (groups,), 0, 2)
    forced = jax.random.randint(key_force, (), 0, groups)
    shared = (flag_draw == 1) | (jnp.arange(groups) == forced)
    shared_block = jnp.repeat(shared, EXPERTS)
    hot_block = jnp.repeat(hot_group, EXPERTS)
    first_expert = perm_table[:, 0]
    swapped = jnp.where(perm_table == hot_block[:, None], first_expert[:, None], perm_table)
    swapped = swapped.at[:, 0].set(hot_block)
    order_table = jnp.where(shared_block[:, None], swapped, perm_table)
    hot_expert = order_table[:, 0]
    others = order_table[:, 1:]
    is_hot = rank_table < CAP
    offset = jnp.where(is_hot, rank_table * (TOPK - 1), CAP * (TOPK - 1) + (rank_table - CAP) * TOPK)
    slot_pos = jnp.arange(TOPK)
    cycle_pos = jnp.where(is_hot[..., None], offset[..., None] + slot_pos - 1, offset[..., None] + slot_pos) % (EXPERTS - 1)
    picked = jnp.take_along_axis(others, cycle_pos.reshape(blocks, TOK_DEV * TOPK), axis=1).reshape(blocks, TOK_DEV, TOPK)
    base_ids = jnp.where(is_hot[..., None] & (slot_pos == 0), hot_expert[:, None, None], picked)
    turn_by = jax.random.randint(key_turn, (blocks, TOK_DEV, 1), 0, TOPK)
    source_pos = (slot_pos - turn_by) % TOPK
    rotated = jnp.take_along_axis(base_ids, source_pos, axis=2)
    return rotated.reshape(TOKENS, TOPK).astype(jnp.int32)


def plant(result, key, smallest, largest):
    longest = result.shape.index(max(result.shape))
    spots = []
    for shift in (0, 1):
        where = [jax.random.randint(jax.random.fold_in(key, axis), (), 0, length) for axis, length in enumerate(result.shape)]
        where[longest] = (where[longest] + shift) % result.shape[longest]
        spots.append(tuple(where))
    return result.at[spots[0]].set(smallest).at[spots[1]].set(largest)


def strengthened(drawn, rng, source, target, parts, factor):
    owner, partner = [(jnp.arange(drawn.shape[dim]) // (drawn.shape[dim] // parts)).reshape([-1 if axis == dim else 1 for axis in range(drawn.ndim)]) for dim in (source, target)]
    chosen = jax.random.permutation(rng, parts)[partner]
    strong = (owner == chosen) | (owner == (partner + parts // 2) % parts)
    return jnp.where(strong, factor * drawn, drawn)


def block_levels(own_key, extent, cuts, low, high):
    level, own = 1.0, jax.random.fold_in(own_key, 6)
    for dim, parts in cuts:
        steps = jnp.exp(jax.random.uniform(jax.random.fold_in(own, dim), (parts,), jnp.float32, low / len(cuts), high / len(cuts)))
        level = level * jnp.repeat(steps, extent[dim] // parts).reshape([-1 if axis == dim else 1 for axis in range(len(extent))])
    return level


def gaussian(rng, shape, width, limit, shards=(), kind=jnp.bfloat16):
    result = width * jax.random.normal(rng, shape, jnp.float32)
    if shards:
        result = result * block_levels(rng, shape, shards, -0.22, 0.18)
    return jnp.clip(result, -limit, limit).astype(kind)


def heavy_noise(own_key, dims, width, most, cuts, heavy, kind=jnp.bfloat16):
    drawn = width * jax.random.normal(own_key, dims, jnp.float32)
    if cuts:
        drawn = drawn * block_levels(own_key, dims, cuts, -0.22, 0.18)
    return jnp.clip(strengthened(drawn, jax.random.fold_in(own_key, 3), *heavy), -most, most).astype(kind)


def setup_inputs(seed: int = 0) -> dict:
    streams_of = jax.random.split(jax.random.key(seed), 11)
    return {
        "tokens": heavy_noise(streams_of[0], (TOKENS, D), 1.0, 24.0, ((0, 512),), (0, 1, 512, 6.0)),
        "out_grad": gaussian(streams_of[1], (TOKENS, D), 0.5, 3.0, ((0, 512),)),
        "expert_ids": draw_expert_ids(jax.random.fold_in(streams_of[10], 71), 0),
        "route_probs": jnp.clip(jnp.exp(math.log(0.8984375) - 2.199401 * jax.random.uniform(streams_of[3], (TOKENS, TOPK), jnp.float32) ** block_levels(streams_of[3], (TOKENS, TOPK), ((0, 512),), -0.2, 0.2)), 0.099609375, 0.8984375).astype(jnp.bfloat16),
        "gate_weight": gaussian(streams_of[4], (EXPERTS, D, HW), D ** -0.5, 0.125, ((0, 32), (1, 16))),
        "up_weight": gaussian(streams_of[5], (EXPERTS, D, HW), D ** -0.5, 0.125, ((0, 32), (1, 16))),
        "down_weight": gaussian(streams_of[6], (EXPERTS, HW, D), HW ** -0.5, 0.3125, ((0, 32), (2, 16))),
        "gate_mask": plant(jax.random.randint(streams_of[7], (EXPERTS, D // 4, HW), 0, 6), jax.random.fold_in(streams_of[7], 1), 0, 5).astype(jnp.int32),
        "up_mask": plant(jax.random.randint(streams_of[8], (EXPERTS, D // 4, HW), 0, 6), jax.random.fold_in(streams_of[8], 1), 0, 5).astype(jnp.int32),
        "down_mask": plant(jax.random.randint(streams_of[9], (EXPERTS, HW // 4, D), 0, 6), jax.random.fold_in(streams_of[9], 1), 0, 5).astype(jnp.int32),
    }


decay_rate = 24.0
pair_table = np.array([[1, 1, 0, 0], [1, 0, 1, 0], [1, 0, 0, 1], [0, 1, 1, 0], [0, 1, 0, 1], [0, 0, 1, 1]], np.float32)


def expand_pattern(pattern):
    group_count, col_count = pattern.shape
    picked = (pattern[None, :, :] == jnp.arange(6, dtype=jnp.int32)[:, None, None]).astype(jnp.float32)
    keeps = jnp.einsum("pgc,pj->gjc", picked, jnp.asarray(pair_table, jnp.float32))
    return keeps.reshape(group_count * 4, col_count)


def expert_slots(flat_ids, expert_count):
    onehot = (flat_ids[..., None] == jnp.arange(expert_count, dtype=jnp.int32)).astype(jnp.int32)
    earlier = jnp.cumsum(onehot, axis=-2) - onehot
    return jnp.sum(earlier * onehot, axis=-1).astype(jnp.int32)


def reference(tokens, out_grad, expert_ids, route_probs, gate_weight, up_weight, down_weight, gate_mask, up_mask, down_mask):
    groups = N_DP
    sources = N_EXPERT
    assigns = TOK_DEV * TOPK
    x_blocks = tokens.reshape(groups, sources, TOK_DEV, D)
    dy_blocks = out_grad.reshape(groups, sources, TOK_DEV, D)
    flat_ids = expert_ids.reshape(groups, sources, assigns)
    flat_probs = route_probs.reshape(groups, sources, assigns)
    slot_index = expert_slots(flat_ids, EXPERTS)
    target = (flat_ids * CAP + slot_index).astype(jnp.int32)
    group_index = jnp.arange(groups, dtype=jnp.int32)[:, None, None]
    source_index = jnp.arange(sources, dtype=jnp.int32)[None, :, None]
    assign_index = jnp.broadcast_to(jnp.arange(assigns, dtype=jnp.int32)[None, None, :], target.shape)
    owner_slot = jnp.full((groups, sources, EXPERTS * CAP), assigns, jnp.int32)
    owner_slot = owner_slot.at[group_index, source_index, target].set(assign_index)

    def one_expert(totals, expert):
        grad_tokens, grad_probs = totals
        picked = lax.dynamic_slice_in_dim(owner_slot, expert * CAP, CAP, 2)
        is_valid = picked < assigns
        assign_pos = jnp.minimum(picked, assigns - 1).astype(jnp.int32)
        token_pos = (assign_pos // TOPK).astype(jnp.int32)
        slot_rows = jnp.take_along_axis(x_blocks, token_pos[..., None], axis=2)
        slot_rows = jnp.where(is_valid[..., None], slot_rows, jnp.zeros_like(slot_rows))
        slot_cotan = jnp.take_along_axis(dy_blocks, token_pos[..., None], axis=2)
        slot_cotan = jnp.where(is_valid[..., None], slot_cotan, jnp.zeros_like(slot_cotan))
        slot_probs = jnp.take_along_axis(flat_probs, assign_pos, axis=2)
        slot_probs = jnp.where(is_valid, slot_probs, jnp.zeros_like(slot_probs))
        keep_gate = expand_pattern(gate_mask[expert])
        keep_up = expand_pattern(up_mask[expert])
        keep_down = expand_pattern(down_mask[expert])
        masked_gate = (gate_weight[expert] * keep_gate).astype(jnp.bfloat16)
        masked_up = (up_weight[expert] * keep_up).astype(jnp.bfloat16)
        masked_down = (down_weight[expert] * keep_down).astype(jnp.bfloat16)
        inputs = slot_rows.reshape(-1, D)
        cotan = slot_cotan.reshape(-1, D)
        probs = slot_probs.reshape(-1)
        gate_pre = jnp.dot(inputs, masked_gate, preferred_element_type=jnp.float32)
        up_pre = jnp.dot(inputs, masked_up, preferred_element_type=jnp.float32)
        sigmoid_val = jax.nn.sigmoid(gate_pre)
        silu_val = gate_pre * sigmoid_val
        hidden = (silu_val * up_pre).astype(jnp.bfloat16)
        expert_out = jnp.dot(hidden, masked_down, preferred_element_type=jnp.float32)
        prob_slot = jnp.sum(expert_out * cotan.astype(jnp.float32), axis=1).astype(jnp.bfloat16)
        weighted = (probs.astype(jnp.float32)[:, None] * cotan.astype(jnp.float32)).astype(jnp.bfloat16)
        hidden_grad = jnp.dot(weighted, masked_down.T, preferred_element_type=jnp.float32)
        gate_delta = (hidden_grad * up_pre * sigmoid_val * (1.0 + gate_pre * (1.0 - sigmoid_val))).astype(jnp.bfloat16)
        up_delta = (hidden_grad * silu_val).astype(jnp.bfloat16)
        slot_grad = (jnp.dot(gate_delta, masked_gate.T, preferred_element_type=jnp.float32)
                     + jnp.dot(up_delta, masked_up.T, preferred_element_type=jnp.float32)).astype(jnp.bfloat16)
        rows_group = inputs.reshape(groups, sources * CAP, D).astype(jnp.float32)
        gate_group = gate_delta.reshape(groups, sources * CAP, HW).astype(jnp.float32)
        up_group = up_delta.reshape(groups, sources * CAP, HW).astype(jnp.float32)
        part_gate = jnp.einsum("grd,grh->gdh", rows_group, gate_group)
        part_up = jnp.einsum("grd,grh->gdh", rows_group, up_group)
        part_gate = lax.optimization_barrier(part_gate.astype(jnp.bfloat16)).astype(jnp.float32)
        part_up = lax.optimization_barrier(part_up.astype(jnp.bfloat16)).astype(jnp.float32)
        gate_total = jnp.sum(part_gate, axis=0) + decay_rate * (1.0 - keep_gate) * gate_weight[expert].astype(jnp.float32)
        up_total = jnp.sum(part_up, axis=0) + decay_rate * (1.0 - keep_up) * up_weight[expert].astype(jnp.float32)
        token_terms = slot_grad.reshape(groups, sources, CAP, D).astype(jnp.float32)
        token_terms = jnp.where(is_valid[..., None], token_terms, jnp.zeros_like(token_terms))
        prob_terms = prob_slot.reshape(groups, sources, CAP).astype(jnp.float32)
        prob_terms = jnp.where(is_valid, prob_terms, jnp.zeros_like(prob_terms))
        grad_tokens = grad_tokens.at[group_index, source_index, token_pos].add(token_terms)
        grad_probs = grad_probs.at[group_index, source_index, assign_pos].add(prob_terms)
        return (grad_tokens, grad_probs), (gate_total, up_total)

    start_tokens = jnp.zeros((groups, sources, TOK_DEV, D), jnp.float32)
    start_probs = jnp.zeros((groups, sources, assigns), jnp.float32)
    finals, grads = lax.scan(one_expert, (start_tokens, start_probs), jnp.arange(EXPERTS, dtype=jnp.int32))
    token_grad = finals[0].astype(jnp.bfloat16).reshape(TOKENS, D)
    prob_grad = finals[1].astype(jnp.bfloat16).reshape(TOKENS, TOPK)
    return (token_grad, prob_grad, grads[0], grads[1])
```

```python
import functools

import jax
import jax.numpy as jnp
from jax import lax
from jax.experimental import pallas as pl
from jax.experimental.pallas import tpu as pltpu
from jax.sharding import PartitionSpec as P

decay_rate = 24.0
main_slots = 8
tail_slots = 4
lane = 128
large = 56
weight_chunks = 4
f32 = jnp.float32
bf16 = jnp.bfloat16
vmem = pl.BlockSpec(memory_space=pltpu.VMEM)
near = pl.BlockSpec(memory_space=pltpu.VMEM)
hbm = pl.BlockSpec(memory_space=pltpu.HBM)
pins = {id(near): pltpu.VMEM, id(hbm): pltpu.HBM}
smem = pl.BlockSpec(memory_space=pltpu.SMEM)


def iota(shape, dim):
    return lax.broadcasted_iota(jnp.int32, shape, dim)


def dot(a, b, dims=((1,), (0,))):
    return lax.dot_general(a, b, (dims, ((), ())), preferred_element_type=f32)


def call(kernel, out_shape, in_specs, out_specs, cost, scratch=(), name=None, mib=12):
    flops, moved = cost

    def run(*args):
        pinned = [
            pltpu.with_memory_space_constraint(x, pins[id(spec)]) if id(spec) in pins else x
            for x, spec in zip(args, in_specs)
        ]
        return kernel_call(*pinned)

    if isinstance(out_specs, tuple):
        out_shape = tuple(
            pins[id(spec)](s.shape, s.dtype) if id(spec) in pins else s
            for s, spec in zip(out_shape, out_specs)
        )
    kernel_call = pl.pallas_call(
        kernel,
        out_shape=out_shape,
        in_specs=in_specs,
        out_specs=out_specs,
        scratch_shapes=scratch,
        compiler_params=pltpu.CompilerParams(vmem_limit_bytes=mib * 1024 * 1024),
        cost_estimate=pl.CostEstimate(flops=flops, bytes_accessed=moved, transcendentals=0),
        name=name,
    )
    return run


def place_kernel(ids_ref, probs_ref, tokens_hbm, grads_hbm, out_hbm, target_ref, tokens, grads, out, sems):
    count, width = tokens.shape
    half = width // 2
    slot_rows = out.shape[0]
    experts = slot_rows // main_slots
    loads = [
        pltpu.make_async_copy(tokens_hbm, tokens, sems.at[0]),
        pltpu.make_async_copy(grads_hbm, grads, sems.at[1]),
    ]
    for load in loads:
        load.start()
    ids = [ids_ref[k : k + 1, :] for k in range(2)]
    named = [(iota((experts, count), 0) == ids[k]).astype(f32) for k in range(2)]
    before = (iota((count, count), 0) < iota((count, count), 1)).astype(bf16)
    earlier = dot((named[0] + named[1]).astype(bf16), before)
    row = iota((slot_rows, count), 0)
    main_hit, tail_hit, targets = [], [], []
    for k in range(2):
        slot = jnp.sum(earlier * named[k], axis=0, keepdims=True).astype(jnp.int32)
        main = jnp.where(slot < main_slots, ids[k] * main_slots + slot, -100)
        tail = jnp.where(slot < main_slots, -100, ids[k] * main_slots + slot - main_slots)
        targets += [main, tail]
        main_hit.append(row == main)
        tail_hit.append((row == tail, row == tail + tail_slots))
    probs = [probs_ref[k : k + 1, :].astype(f32) for k in range(2)]
    target_ref[...] = jnp.concatenate([t.astype(f32) for t in targets] + probs + probs, axis=0)

    def placing(hit, scale):
        return (jnp.where(hit[0], scale[0], 0.0) + jnp.where(hit[1], scale[1], 0.0)).astype(bf16)

    stores = []

    def store(start, size):
        span = (slice(None), pl.ds(start, size))
        sem = sems.at[2 + len(stores)]
        stores.append(pltpu.make_async_copy(out.at[span], out_hbm.at[span], sem))
        stores[-1].start()

    for at, (source, scale) in enumerate(((tokens, (1.0, 1.0)), (grads, probs))):
        base = at * (width + half)
        main = placing(main_hit, scale)
        tail = jnp.concatenate(
            [placing([tail_hit[k][side] for k in range(2)], scale) for side in range(2)], axis=1
        )
        loads[at].wait()
        out[:, base : base + width] = dot(main, source[...]).astype(bf16)
        store(base, width)
        halves = jnp.concatenate([source[:, :half], source[:, half:]], axis=0)
        out[:, base + width : base + width + half] = dot(tail, halves).astype(bf16)
        store(base + width, half)
    for copy in stores:
        copy.wait()


def kept(pattern_ref):
    groups = pattern_ref.shape[0]
    rows = groups * 4
    spread = (iota((rows, groups), 0) // 4 == iota((rows, groups), 1)).astype(bf16)
    p = dot(spread, pattern_ref[...].astype(f32).astype(bf16))
    j = iota(p.shape, 0) % 4
    one = (p == 0.0) | (p == 3.0) | (p == 4.0)
    two = (p == 1.0) | (p == 3.0) | (p == 5.0)
    three = (p == 2.0) | (p >= 4.0)
    keep = ((j == 0) & (p <= 2.0)) | ((j == 1) & one) | ((j == 2) & two) | ((j == 3) & three)
    return keep


def mask_kernel(
    gate_ref, up_ref, down_ref, gate_mask_ref, up_mask_ref, down_mask_ref, out_ref, decay_ref
):
    hidden = gate_ref.shape[1]
    for at, (weight, mask) in enumerate(((gate_ref, gate_mask_ref), (up_ref, up_mask_ref))):
        span = slice(at * hidden, (at + 1) * hidden)
        keep, dense = kept(mask), weight[...].astype(f32)
        out_ref[:, span] = jnp.where(keep, dense, 0.0).astype(bf16)
        decay_ref[:, span] = jnp.where(keep, 0.0, decay_rate * dense)
    masked = jnp.where(kept(down_mask_ref), down_ref[...].astype(f32), 0.0)
    out_ref[:, 2 * hidden :] = masked.T.astype(bf16)


def tail_sides(rows):
    wide = rows * main_slots // tail_slots
    r = iota((rows, wide), 0)
    low = r // tail_slots * main_slots + r % tail_slots
    c = iota((rows, wide), 1)
    return (c == low).astype(bf16), (c == low + tail_slots).astype(bf16)


def tail_sides_t(rows):
    wide = rows * main_slots // tail_slots
    r = iota((wide, rows), 1)
    low = r // tail_slots * main_slots + r % tail_slots
    c = iota((wide, rows), 0)
    return (c == low).astype(bf16), (c == low + tail_slots).astype(bf16)


def assemble_kernel(order, place_ref, target_ref, *refs):
    pieces = 2 * len(order)
    piece_refs = refs[:pieces]
    weight_hbm, left_ref, right_ref, weight, sems = refs[pieces:]
    depth = piece_refs[0].shape[0]
    y, core = place_ref[0], place_ref[1]
    copies = []
    for k in range(pieces):
        origin = lax.rem(y + (len(order) - order[k % len(order)]), len(order))
        offset = (2 * origin + (core if k < len(order) else 1 - core)) * depth
        to = weight.at[pl.ds(pl.multiple_of(offset, depth), depth)]
        copies.append(pltpu.make_async_copy(piece_refs[k], to, sems.at[k]))
        copies[-1].start()
    count = target_ref.shape[1]
    slot_rows = left_ref.shape[1] // 2
    row = iota((slot_rows, count), 0).astype(f32)
    main0, tail0, main1, tail1 = [target_ref[k : k + 1, :] for k in range(4)]
    main = ((row == main0) | (row == main1)).astype(f32).T.astype(bf16)
    low = ((row == tail0) | (row == tail1)).astype(f32).T.astype(bf16)
    high = ((row == tail0 + tail_slots) | (row == tail1 + tail_slots)).astype(f32).T.astype(bf16)
    left_ref[:, :slot_rows] = main
    left_ref[:, slot_rows:] = low
    right_ref[:, :slot_rows] = main
    right_ref[:, slot_rows:] = high
    for copy in copies:
        copy.wait()
    store = pltpu.make_async_copy(weight, weight_hbm, sems.at[pieces])
    store.start()
    store.wait()


def weight_grads(place_ref, delta_t_ref, rows_ref, out, own, after):
    steps = out.shape[0]
    y, core = place_ref[0], place_ref[1]
    side = (core if own else 1 - core) * lane

    def columns(d):
        at = lax.rem(y + d, steps) * 2 * lane + side
        return rows_ref[:, pl.ds(pl.multiple_of(at, lane), lane)]

    for d in range(0, steps, 2):
        part = dot(delta_t_ref[...], jnp.concatenate([columns(d), columns(d + 1)], axis=1))
        out[d] = part[:, :lane].astype(bf16)
        out[d + 1] = part[:, lane:].astype(bf16)
        after(d)


def delta_kernel(
    place_ref,
    x_ref,
    weight_hbm,
    delta_ref,
    prob_ref,
    delta_t_ref,
    rows,
    weight,
    other_hbm,
    down,
    cotan,
    other,
    sems,
    load_sems,
):
    width, hidden = down.shape
    half = width // 2
    depth = width // weight_chunks
    spans = [slice(k * depth, (k + 1) * depth) for k in range(weight_chunks)]
    loads = [
        pltpu.make_async_copy(weight_hbm.at[span, pl.ds(0, 2 * hidden)], weight.at[span], load_sems.at[k])
        for k, span in enumerate(spans)
    ]
    loads.append(
        pltpu.make_async_copy(
            weight_hbm.at[:, pl.ds(2 * hidden, hidden)], down, load_sems.at[weight_chunks]
        )
    )
    for load in loads:
        load.start()
    main_rows = x_ref.shape[0]
    tail_rows = main_rows * tail_slots // main_slots
    low, high = tail_sides(tail_rows)
    for at, target in enumerate((rows, cotan)):
        base = at * (width + half)
        target[:main_rows, :] = x_ref[:, base : base + width]
        halves = x_ref[:, base + width : base + width + half]
        target[main_rows:, :half] = dot(low, halves).astype(bf16)
        target[main_rows:, half:] = dot(high, halves).astype(bf16)
    pre = 0.0
    for load, span in zip(loads, spans):
        load.wait()
        pre = pre + dot(rows[:, span], weight[span, :])
    loads[-1].wait()
    grad = dot(cotan[...], down[...])
    gate_pre, up_pre = pre[:, :hidden], pre[:, hidden:]
    sig = jax.nn.sigmoid(gate_pre)
    silu = gate_pre * sig
    act = (silu * up_pre).astype(bf16)
    prob = jnp.sum(act.astype(f32) * grad, axis=1, keepdims=True)
    prob_ref[...] = jnp.broadcast_to(prob, prob_ref.shape).astype(bf16)
    gate_delta = (grad * up_pre * sig * (1.0 + gate_pre * (1.0 - sig))).astype(bf16)
    up_delta = (grad * silu).astype(bf16)
    delta_ref[:, :hidden] = gate_delta
    delta_ref[:, hidden:] = up_delta
    delta_t_ref[:hidden, :] = gate_delta.T
    delta_t_ref[hidden:, :] = up_delta.T
    stores = []

    def after(d):
        span = pl.ds(d, 2)
        stores.append(pltpu.make_async_copy(other.at[span], other_hbm.at[span], sems.at[d // 2]))
        stores[-1].start()

    weight_grads(place_ref, delta_t_ref, rows, other, False, after)
    for copy in stores:
        copy.wait()


def slot_grad_kernel(
    place_ref, delta_ref, prob_ref, delta_t_ref, rows_ref, weight_ref, out_hbm, mine_ref, out, sems
):
    width = weight_ref.shape[0]
    half = width // 2
    main_rows = out.shape[0]
    tail_rows = delta_ref.shape[0] - main_rows
    stores = []

    def store(start, size):
        span = (slice(None), pl.ds(start, size))
        sem = sems.at[len(stores)]
        stores.append(pltpu.make_async_copy(out.at[span], out_hbm.at[span], sem))
        stores[-1].start()

    low_t, high_t = tail_sides_t(tail_rows)
    tails = []
    for at in range(2):
        span = slice(at * half, (at + 1) * half)
        back = dot(delta_ref[...], weight_ref[span, :], ((1,), (1,))).astype(bf16)
        out[:, span] = back[:main_rows]
        store(at * half, half)
        tails.append(back[main_rows:])
    tail = dot(low_t, tails[0]) + dot(high_t, tails[1])
    out[:, width : width + half] = tail.astype(bf16)
    at_lane = iota((main_rows, lane), 1)
    late = dot(low_t, prob_ref[main_rows:, :])
    probs = jnp.where(at_lane == 1, late, prob_ref[:main_rows, :].astype(f32))
    out[:, width + half :] = probs.astype(bf16)
    store(width, half + lane)
    weight_grads(place_ref, delta_t_ref, rows_ref, mine_ref, True, lambda d: None)
    for copy in stores:
        copy.wait()


def pair_sum_kernel(mine_ref, got_ref, *refs):
    steps = mine_ref.shape[0]
    outs, sums, sems = refs[:steps], refs[steps], refs[steps + 1]
    stores = []
    for d, out in enumerate(outs):
        sums[d] = (mine_ref[d].astype(f32) + got_ref[d].astype(f32)).astype(bf16)
        stores.append(pltpu.make_async_copy(sums.at[d], out, sems.at[d]))
        stores[-1].start()
    for copy in stores:
        copy.wait()


def finish_weights_kernel(decay_ref, *refs):
    gate_out, up_out = refs[-2:]
    hidden = gate_out.shape[1]
    total = refs[0][...].astype(f32)
    for ref in refs[1:-2]:
        total = total + ref[...].astype(f32)
    total = total.T + decay_ref[...]
    gate_out[...] = total[:, :hidden]
    up_out[...] = total[:, hidden:]


def finish_tokens_kernel(target_ref, left_ref, right_ref, back_ref, grad_ref, prob_ref):
    width = grad_ref.shape[1]
    half = width // 2
    slot_rows = back_ref.shape[0]
    tail = back_ref[:, width : width + half]
    for at, place in enumerate((left_ref, right_ref)):
        span = slice(at * half, (at + 1) * half)
        stacked = jnp.concatenate([back_ref[:, span], tail], axis=0)
        grad_ref[:, span] = dot(place[...], stacked).astype(bf16)
    returned = back_ref[:, width + half :].astype(f32)
    row = iota((slot_rows, target_ref.shape[1]), 0).astype(f32)
    for k in range(2):
        main, late = target_ref[2 * k : 2 * k + 1, :], target_ref[2 * k + 1 : 2 * k + 2, :]
        picked = jnp.where(row == main, returned[:, 0:1], 0.0)
        picked = picked + jnp.where(row == late, returned[:, 1:2], 0.0)
        total = jnp.sum(picked, axis=0, keepdims=True)
        prob_ref[k : k + 1, :] = (total / target_ref[4 + k : 5 + k, :]).astype(bf16)


def per_device(
    tokens,
    out_grad,
    expert_ids,
    route_probs,
    gate_weight,
    up_weight,
    down_weight,
    gate_mask,
    up_mask,
    down_mask,
):
    count, width = tokens.shape
    half = width // 2
    hidden = gate_weight.shape[2]
    experts = lax.axis_size("expert")
    dp = lax.axis_size("dp")
    ny = dp // 2
    slot_rows = experts * main_slots
    all_rows = experts * (main_slots + tail_slots)
    me = lax.axis_index("dp")
    here = jnp.stack([lax.shift_right_logical(me, 1), lax.bitwise_and(me, 1)])
    sds = jax.ShapeDtypeStruct
    ids, probs = expert_ids.T, route_probs.T

    sent, targets = call(
        place_kernel,
        (sds((slot_rows, 3 * width), bf16), sds((8, count), f32)),
        [vmem, vmem, hbm, hbm],
        (hbm, vmem),
        (slot_rows * count * width * 10, 5 * slot_rows * width * 2),
        scratch=(
            pltpu.VMEM((count, width), bf16),
            pltpu.VMEM((count, width), bf16),
            pltpu.VMEM((slot_rows, 3 * width), bf16),
            pltpu.SemaphoreType.DMA((6,)),
        ),
        name="place",
        mib=large,
    )(ids, probs, tokens, out_grad)

    def exchange(x):
        blocks = x.reshape(experts, main_slots, x.shape[1])
        moved = lax.all_to_all(blocks, "expert", split_axis=0, concat_axis=0, tiled=True)
        return moved.reshape(x.shape)

    arrived = exchange(sent)

    piece, decay = call(
        mask_kernel,
        (sds((width // dp, 3 * hidden), bf16), sds((width // dp, 2 * hidden), f32)),
        [vmem] * 6,
        (vmem, vmem),
        (width * hidden * 100, 6 * width // dp * hidden),
        name="mask",
        mib=large,
    )(gate_weight[0], up_weight[0], down_weight[0], gate_mask[0], up_mask[0], down_mask[0])

    def along_y(x, d):
        moves = [(2 * a + c, 2 * ((a + d) % ny) + c) for a in range(ny) for c in range(2)]
        return lax.ppermute(x, "dp", moves)

    def across(x):
        return lax.ppermute(x, "dp", [(i, i ^ 1) for i in range(dp)])

    forward, backward = [piece], [piece]
    for _ in range(ny // 2):
        forward.append(along_y(forward[-1], 1))
        backward.append(along_y(backward[-1], ny - 1))
    held = [(0, piece)] + [(d, forward[d]) for d in range(1, ny // 2 + 1)]
    held += [(ny - d, backward[d]) for d in range(1, ny // 2)]
    other = [across(x) for _, x in held]
    weights, place_left, place_right = call(
        functools.partial(assemble_kernel, [d for d, _ in held]),
        (sds((width, 3 * hidden), bf16),) + (sds((count, 2 * slot_rows), bf16),) * 2,
        [smem, vmem] + [hbm] * dp,
        (hbm, vmem, vmem),
        (count * slot_rows * 10, 6 * width * hidden),
        scratch=(
            pltpu.VMEM((width, 3 * hidden), bf16),
            pltpu.SemaphoreType.DMA((dp + 1,)),
        ),
        name="assemble",
    )(here, targets, *[x for _, x in held], *other)

    block = (2 * hidden, lane)
    delta, slot_probs, delta_t, rows, gate_up, theirs = call(
        delta_kernel,
        (
            sds((all_rows, 2 * hidden), bf16),
            sds((all_rows, lane), bf16),
            sds((2 * hidden, all_rows), bf16),
            sds((all_rows, width), bf16),
            sds((width, 2 * hidden), bf16),
            sds((ny, *block), bf16),
        ),
        [smem, vmem, hbm],
        (near,) * 5 + (hbm,),
        (all_rows * width * hidden * 8, 12 * slot_rows * width),
        scratch=(
            pltpu.VMEM((width, hidden), bf16),
            pltpu.VMEM((all_rows, width), bf16),
            pltpu.VMEM((ny, *block), bf16),
            pltpu.SemaphoreType.DMA((ny // 2,)),
            pltpu.SemaphoreType.DMA((weight_chunks + 1,)),
        ),
        name="delta",
        mib=24,
    )(here, arrived, weights)
    got = across(theirs)
    returned, mine = call(
        slot_grad_kernel,
        (sds((slot_rows, width + half + lane), bf16), sds((ny, *block), bf16)),
        [smem] + [near] * 5,
        (hbm, near),
        (all_rows * width * hidden * 6, 12 * slot_rows * width),
        scratch=(
            pltpu.VMEM((slot_rows, width + half + lane), bf16),
            pltpu.SemaphoreType.DMA((3,)),
        ),
        name="slot_grad",
        mib=24,
    )(here, delta, slot_probs, delta_t, rows, gate_up)
    sums = call(
        pair_sum_kernel,
        (sds(block, bf16),) * ny,
        [near, vmem],
        (hbm,) * ny,
        (width * hidden * 2, 12 * width * hidden),
        scratch=(pltpu.VMEM((ny, *block), bf16), pltpu.SemaphoreType.DMA((ny,))),
        name="pair_sum",
    )(mine, got)
    returned, *sums = lax.optimization_barrier((returned, *sums))
    back = exchange(returned)
    far_first = sorted(range(1, ny), key=lambda d: -min(d, ny - d))
    terms = [sums[0]] + [along_y(sums[d], d) for d in far_first]
    gate_grad, up_grad = call(
        finish_weights_kernel,
        (sds((width // dp, hidden), f32),) * 2,
        [vmem] * (1 + ny),
        (vmem, vmem),
        (width * hidden * 2, 4 * width * hidden),
        name="finish_weights",
    )(decay, *terms)
    token_grad, prob_grad = call(
        finish_tokens_kernel,
        (sds((count, width), bf16), sds((2, count), bf16)),
        [vmem] * 4,
        (vmem, vmem),
        (count * slot_rows * width * 4, 6 * slot_rows * width),
        name="finish_tokens",
        mib=16,
    )(targets, place_left, place_right, back)
    return token_grad, prob_grad.T, gate_grad[None], up_grad[None]


def solution(mesh):
    placed = (
        P(("dp", "expert"), None),
        P(("dp", "expert"), None),
        P(("dp", "expert"), None),
        P(("dp", "expert"), None),
        P("expert", "dp", None),
        P("expert", "dp", None),
        P("expert", None, "dp"),
        P("expert", "dp", None),
        P("expert", "dp", None),
        P("expert", None, "dp"),
    )
    return jax.shard_map(
        per_device,
        mesh=mesh,
        in_specs=placed,
        out_specs=(
            P(("dp", "expert"), None),
            P(("dp", "expert"), None),
            P("expert", "dp", None),
            P("expert", "dp", None),
        ),
        check_vma=False,
    )
```

```python
import functools

import jax
import jax.numpy as jnp
from jax import lax
from jax.experimental import pallas as pl
from jax.experimental.pallas import tpu as pltpu
from jax.sharding import PartitionSpec as P

decay_rate = 24.0
main_slots = 8
tail_slots = 4
lane = 128
large = 56
weight_chunks = 4
f32 = jnp.float32
bf16 = jnp.bfloat16
vmem = pl.BlockSpec(memory_space=pltpu.VMEM)
near = pl.BlockSpec(memory_space=pltpu.VMEM)
hbm = pl.BlockSpec(memory_space=pltpu.HBM)
pins = {id(near): pltpu.VMEM, id(hbm): pltpu.HBM}


def iota(shape, dim):
    return lax.broadcasted_iota(jnp.int32, shape, dim)


def position():
    me = lax.axis_index("dp")
    return lax.shift_right_logical(me, 1), lax.bitwise_and(me, 1)


def dot(a, b, dims=((1,), (0,))):
    return lax.dot_general(a, b, (dims, ((), ())), preferred_element_type=f32)


def call(kernel, out_shape, in_specs, out_specs, cost, scratch=(), name=None, mib=12):
    flops, moved = cost

    def run(*args):
        pinned = [
            pltpu.with_memory_space_constraint(x, pins[id(spec)]) if id(spec) in pins else x
            for x, spec in zip(args, in_specs)
        ]
        return kernel_call(*pinned)

    if isinstance(out_specs, tuple):
        out_shape = tuple(
            pins[id(spec)](s.shape, s.dtype) if id(spec) in pins else s
            for s, spec in zip(out_shape, out_specs)
        )
    kernel_call = pl.pallas_call(
        kernel,
        out_shape=out_shape,
        in_specs=in_specs,
        out_specs=out_specs,
        scratch_shapes=scratch,
        compiler_params=pltpu.CompilerParams(vmem_limit_bytes=mib * 1024 * 1024),
        cost_estimate=pl.CostEstimate(flops=flops, bytes_accessed=moved, transcendentals=0),
        name=name,
    )
    return run


def place_kernel(
    ids_hbm, probs_hbm, tokens_hbm, grads_hbm, out_hbm, target_hbm, ids_ref, probs_ref, tokens, grads, out, target, sems
):
    count, width = tokens.shape
    half = width // 2
    slot_rows = out.shape[0]
    experts = slot_rows // main_slots
    parts = ((ids_hbm, ids_ref), (probs_hbm, probs_ref), (tokens_hbm, tokens), (grads_hbm, grads))
    loads = [pltpu.make_async_copy(x, y, sems.at[k]) for k, (x, y) in enumerate(parts)]
    for load in loads:
        load.start()
    loads[0].wait()
    loads[1].wait()
    ids = [ids_ref[k : k + 1, :] for k in range(2)]
    named = [(iota((experts, count), 0) == ids[k]).astype(f32) for k in range(2)]
    before = (iota((count, count), 0) < iota((count, count), 1)).astype(bf16)
    earlier = dot((named[0] + named[1]).astype(bf16), before)
    row = iota((slot_rows, count), 0)
    main_hit, tail_hit, targets = [], [], []
    for k in range(2):
        slot = jnp.sum(earlier * named[k], axis=0, keepdims=True).astype(jnp.int32)
        main = jnp.where(slot < main_slots, ids[k] * main_slots + slot, -100)
        tail = jnp.where(slot < main_slots, -100, ids[k] * main_slots + slot - main_slots)
        targets += [main, tail]
        main_hit.append(row == main)
        tail_hit.append((row == tail, row == tail + tail_slots))
    probs = [probs_ref[k : k + 1, :].astype(f32) for k in range(2)]
    target[...] = jnp.concatenate([t.astype(f32) for t in targets] + probs + probs, axis=0)
    stores = [pltpu.make_async_copy(target, target_hbm, sems.at[4])]
    stores[0].start()

    def placing(hit, scale):
        return (jnp.where(hit[0], scale[0], 0.0) + jnp.where(hit[1], scale[1], 0.0)).astype(bf16)

    def store(start, size):
        span = (slice(None), pl.ds(start, size))
        sem = sems.at[4 + len(stores)]
        stores.append(pltpu.make_async_copy(out.at[span], out_hbm.at[span], sem))
        stores[-1].start()

    for at, (source, scale) in enumerate(((tokens, (1.0, 1.0)), (grads, probs))):
        base = at * (width + half)
        main = placing(main_hit, scale)
        tail = jnp.concatenate(
            [placing([tail_hit[k][side] for k in range(2)], scale) for side in range(2)], axis=1
        )
        loads[2 + at].wait()
        out[:, base : base + width] = dot(main, source[...]).astype(bf16)
        store(base, width)
        halves = jnp.concatenate([source[:, :half], source[:, half:]], axis=0)
        out[:, base + width : base + width + half] = dot(tail, halves).astype(bf16)
        store(base + width, half)
    for copy in stores:
        copy.wait()


def kept(pattern_ref):
    groups = pattern_ref.shape[0]
    rows = groups * 4
    spread = (iota((rows, groups), 0) // 4 == iota((rows, groups), 1)).astype(bf16)
    p = dot(spread, pattern_ref[...].astype(f32).astype(bf16))
    j = iota(p.shape, 0) % 4
    one = (p == 0.0) | (p == 3.0) | (p == 4.0)
    two = (p == 1.0) | (p == 3.0) | (p == 5.0)
    three = (p == 2.0) | (p >= 4.0)
    keep = ((j == 0) & (p <= 2.0)) | ((j == 1) & one) | ((j == 2) & two) | ((j == 3) & three)
    return keep


def mask_kernel(
    gate_ref, up_ref, down_ref, gate_mask_ref, up_mask_ref, down_mask_ref, out_ref, decay_ref
):
    hidden = gate_ref.shape[1]
    for at, (weight, mask) in enumerate(((gate_ref, gate_mask_ref), (up_ref, up_mask_ref))):
        span = slice(at * hidden, (at + 1) * hidden)
        keep, dense = kept(mask), weight[...].astype(f32)
        out_ref[:, span] = jnp.where(keep, dense, 0.0).astype(bf16)
        decay_ref[:, span] = jnp.where(keep, 0.0, decay_rate * dense)
    masked = jnp.where(kept(down_mask_ref), down_ref[...].astype(f32), 0.0)
    out_ref[:, 2 * hidden :] = masked.T.astype(bf16)


def tail_sides(rows):
    wide = rows * main_slots // tail_slots
    r = iota((rows, wide), 0)
    low = r // tail_slots * main_slots + r % tail_slots
    c = iota((rows, wide), 1)
    return (c == low).astype(bf16), (c == low + tail_slots).astype(bf16)


def tail_sides_t(rows):
    wide = rows * main_slots // tail_slots
    r = iota((wide, rows), 1)
    low = r // tail_slots * main_slots + r % tail_slots
    c = iota((wide, rows), 0)
    return (c == low).astype(bf16), (c == low + tail_slots).astype(bf16)


def assemble_kernel(order, target_ref, *refs):
    pieces = 2 * len(order)
    piece_refs = refs[:pieces]
    weight_hbm, down_hbm, turned_hbm, left_ref, right_ref, weight, turned, sems = refs[pieces:]
    depth = piece_refs[0].shape[0]
    y, core = position()
    copies = []
    for k in range(pieces):
        origin = lax.rem(y + (len(order) - order[k % len(order)]), len(order))
        offset = (2 * origin + (core if k < len(order) else 1 - core)) * depth
        to = weight.at[pl.ds(pl.multiple_of(offset, depth), depth)]
        copies.append(pltpu.make_async_copy(piece_refs[k], to, sems.at[k]))
        copies[-1].start()
    count = target_ref.shape[1]
    slot_rows = left_ref.shape[1] // 2
    row = iota((slot_rows, count), 0).astype(f32)
    main0, tail0, main1, tail1 = [target_ref[k : k + 1, :] for k in range(4)]
    main = ((row == main0) | (row == main1)).astype(f32).T.astype(bf16)
    low = ((row == tail0) | (row == tail1)).astype(f32).T.astype(bf16)
    high = ((row == tail0 + tail_slots) | (row == tail1 + tail_slots)).astype(f32).T.astype(bf16)
    left_ref[:, :slot_rows] = main
    left_ref[:, slot_rows:] = low
    right_ref[:, :slot_rows] = main
    right_ref[:, slot_rows:] = high
    for copy in copies:
        copy.wait()
    gate_up = turned.shape[0]
    stores = [
        pltpu.make_async_copy(weight.at[:, pl.ds(0, gate_up)], weight_hbm, sems.at[0]),
        pltpu.make_async_copy(weight.at[:, pl.ds(gate_up, gate_up // 2)], down_hbm, sems.at[1]),
        pltpu.make_async_copy(turned, turned_hbm, sems.at[2]),
    ]
    stores[0].start()
    stores[1].start()
    for at in range(0, turned.shape[1], 2 * lane):
        turned[:, at : at + 2 * lane] = weight[at : at + 2 * lane, :gate_up].T
    stores[2].start()
    for store in stores:
        store.wait()


def weight_grads(delta_t_ref, rows_ref, out, own, after):
    steps = out.shape[0]
    y, core = position()
    side = (core if own else 1 - core) * lane

    def columns(d):
        at = lax.rem(y + d, steps) * 2 * lane + side
        return rows_ref[:, pl.ds(pl.multiple_of(at, lane), lane)]

    for d in range(0, steps, 2):
        part = dot(delta_t_ref[...], jnp.concatenate([columns(d), columns(d + 1)], axis=1))
        out[d] = part[:, :lane].astype(bf16)
        out[d + 1] = part[:, lane:].astype(bf16)
        after(d)


def delta_kernel(
    x_ref,
    weight_hbm,
    down_hbm,
    turned_hbm,
    delta_ref,
    prob_ref,
    turned,
    mine_ref,
    other_hbm,
    delta_t_ref,
    rows,
    weight,
    down,
    cotan,
    other,
    sems,
    load_sems,
):
    width, hidden = down.shape
    half = width // 2
    depth = width // weight_chunks
    spans = [slice(k * depth, (k + 1) * depth) for k in range(weight_chunks)]
    loads = [
        pltpu.make_async_copy(weight_hbm.at[span], weight.at[span], load_sems.at[k])
        for k, span in enumerate(spans)
    ]
    loads.append(pltpu.make_async_copy(down_hbm, down, load_sems.at[weight_chunks]))
    loads.append(pltpu.make_async_copy(turned_hbm, turned, load_sems.at[weight_chunks + 1]))
    for load in loads:
        load.start()
    main_rows = x_ref.shape[0]
    tail_rows = main_rows * tail_slots // main_slots
    low, high = tail_sides(tail_rows)
    for at, target in enumerate((rows, cotan)):
        base = at * (width + half)
        target[:main_rows, :] = x_ref[:, base : base + width]
        halves = x_ref[:, base + width : base + width + half]
        target[main_rows:, :half] = dot(low, halves).astype(bf16)
        target[main_rows:, half:] = dot(high, halves).astype(bf16)
    pre = 0.0
    for load, span in zip(loads, spans):
        load.wait()
        pre = pre + dot(rows[:, span], weight[span, :])
    loads[-2].wait()
    grad = dot(cotan[...], down[...])
    gate_pre, up_pre = pre[:, :hidden], pre[:, hidden:]
    sig = jax.nn.sigmoid(gate_pre)
    silu = gate_pre * sig
    act = (silu * up_pre).astype(bf16)
    prob = jnp.sum(act.astype(f32) * grad, axis=1, keepdims=True)
    prob_ref[...] = jnp.broadcast_to(prob, prob_ref.shape).astype(bf16)
    gate_delta = (grad * up_pre * sig * (1.0 + gate_pre * (1.0 - sig))).astype(bf16)
    up_delta = (grad * silu).astype(bf16)
    delta_ref[:, :hidden] = gate_delta
    delta_ref[:, hidden:] = up_delta
    delta_t_ref[:hidden, :] = gate_delta.T
    delta_t_ref[hidden:, :] = up_delta.T
    stores = []

    def after(d):
        span = pl.ds(d, 2)
        stores.append(pltpu.make_async_copy(other.at[span], other_hbm.at[span], sems.at[d // 2]))
        stores[-1].start()

    weight_grads(delta_t_ref, rows, other, False, after)
    weight_grads(delta_t_ref, rows, mine_ref, True, lambda d: None)
    for copy in stores + loads[-1:]:
        copy.wait()


def slot_grad_kernel(delta_ref, prob_ref, turned_ref, out_hbm, out, sems):
    width = turned_ref.shape[1]
    half = width // 2
    main_rows = out.shape[0]
    tail_rows = delta_ref.shape[0] - main_rows
    stores = []

    def store(start, size):
        span = (slice(None), pl.ds(start, size))
        sem = sems.at[len(stores)]
        stores.append(pltpu.make_async_copy(out.at[span], out_hbm.at[span], sem))
        stores[-1].start()

    low_t, high_t = tail_sides_t(tail_rows)
    tails = []
    for at in range(2):
        span = slice(at * half, (at + 1) * half)
        back = dot(delta_ref[...], turned_ref[:, span]).astype(bf16)
        out[:, span] = back[:main_rows]
        store(at * half, half)
        tails.append(back[main_rows:])
    tail = dot(low_t, tails[0]) + dot(high_t, tails[1])
    out[:, width : width + half] = tail.astype(bf16)
    at_lane = iota((main_rows, lane), 1)
    late = dot(low_t, prob_ref[main_rows:, :])
    probs = jnp.where(at_lane == 1, late, prob_ref[:main_rows, :].astype(f32))
    out[:, width + half :] = probs.astype(bf16)
    store(width, half + lane)
    for copy in stores:
        copy.wait()


def pair_sum_kernel(mine_ref, got_ref, *refs):
    steps = mine_ref.shape[0]
    outs, sums, sems = refs[:steps], refs[steps], refs[steps + 1]
    stores = []
    for d, out in enumerate(outs):
        sums[d] = (mine_ref[d].astype(f32) + got_ref[d].astype(f32)).astype(bf16)
        stores.append(pltpu.make_async_copy(sums.at[d], out, sems.at[d]))
        stores[-1].start()
    for copy in stores:
        copy.wait()


def finish_weights_kernel(decay_ref, *refs):
    gate_out, up_out = refs[-2:]
    hidden = gate_out.shape[1]
    total = refs[0][...].astype(f32)
    for ref in refs[1:-2]:
        total = total + ref[...].astype(f32)
    total = total.T + decay_ref[...]
    gate_out[...] = total[:, :hidden]
    up_out[...] = total[:, hidden:]


def finish_tokens_kernel(target_ref, left_ref, right_ref, back_ref, grad_ref, prob_ref):
    width = grad_ref.shape[1]
    half = width // 2
    slot_rows = back_ref.shape[0]
    tail = back_ref[:, width : width + half]
    for at, place in enumerate((left_ref, right_ref)):
        span = slice(at * half, (at + 1) * half)
        stacked = jnp.concatenate([back_ref[:, span], tail], axis=0)
        grad_ref[:, span] = dot(place[...], stacked).astype(bf16)
    returned = back_ref[:, width + half :].astype(f32)
    row = iota((slot_rows, target_ref.shape[1]), 0).astype(f32)
    for k in range(2):
        main, late = target_ref[2 * k : 2 * k + 1, :], target_ref[2 * k + 1 : 2 * k + 2, :]
        picked = jnp.where(row == main, returned[:, 0:1], 0.0)
        picked = picked + jnp.where(row == late, returned[:, 1:2], 0.0)
        total = jnp.sum(picked, axis=0, keepdims=True)
        prob_ref[k : k + 1, :] = (total / target_ref[4 + k : 5 + k, :]).astype(bf16)


def per_device(
    tokens,
    out_grad,
    expert_ids,
    route_probs,
    gate_weight,
    up_weight,
    down_weight,
    gate_mask,
    up_mask,
    down_mask,
):
    count, width = tokens.shape
    half = width // 2
    hidden = gate_weight.shape[2]
    experts = lax.axis_size("expert")
    dp = lax.axis_size("dp")
    ny = dp // 2
    slot_rows = experts * main_slots
    all_rows = experts * (main_slots + tail_slots)
    sds = jax.ShapeDtypeStruct
    ids, probs = expert_ids.T, route_probs.T

    sent, targets = call(
        place_kernel,
        (sds((slot_rows, 3 * width), bf16), sds((8, count), f32)),
        [hbm] * 4,
        (hbm, hbm),
        (slot_rows * count * width * 10, 5 * slot_rows * width * 2),
        scratch=(
            pltpu.VMEM((2, count), jnp.int32),
            pltpu.VMEM((2, count), bf16),
            pltpu.VMEM((count, width), bf16),
            pltpu.VMEM((count, width), bf16),
            pltpu.VMEM((slot_rows, 3 * width), bf16),
            pltpu.VMEM((8, count), f32),
            pltpu.SemaphoreType.DMA((9,)),
        ),
        name="place",
        mib=large,
    )(ids, probs, tokens, out_grad)

    def exchange(x):
        blocks = x.reshape(experts, main_slots, x.shape[1])
        moved = lax.all_to_all(blocks, "expert", split_axis=0, concat_axis=0, tiled=True)
        return moved.reshape(x.shape)

    arrived = exchange(sent)

    piece, decay = call(
        mask_kernel,
        (sds((width // dp, 3 * hidden), bf16), sds((width // dp, 2 * hidden), f32)),
        [vmem] * 6,
        (vmem, vmem),
        (width * hidden * 100, 6 * width // dp * hidden),
        name="mask",
        mib=large,
    )(gate_weight[0], up_weight[0], down_weight[0], gate_mask[0], up_mask[0], down_mask[0])

    def along_y(x, d):
        moves = [(2 * a + c, 2 * ((a + d) % ny) + c) for a in range(ny) for c in range(2)]
        return lax.ppermute(x, "dp", moves)

    def across(x):
        return lax.ppermute(x, "dp", [(i, i ^ 1) for i in range(dp)])

    forward, backward = [piece], [piece]
    for _ in range(ny // 2):
        forward.append(along_y(forward[-1], 1))
        backward.append(along_y(backward[-1], ny - 1))
    held = [(0, piece)] + [(d, forward[d]) for d in range(1, ny // 2 + 1)]
    held += [(ny - d, backward[d]) for d in range(1, ny // 2)]
    other = [across(x) for _, x in held]
    gate_up, down, turned, place_left, place_right = call(
        functools.partial(assemble_kernel, [d for d, _ in held]),
        (
            sds((width, 2 * hidden), bf16),
            sds((width, hidden), bf16),
            sds((2 * hidden, width), bf16),
        )
        + (sds((count, 2 * slot_rows), bf16),) * 2,
        [vmem] + [hbm] * dp,
        (hbm, hbm, hbm, vmem, vmem),
        (count * slot_rows * 10, 6 * width * hidden),
        scratch=(
            pltpu.VMEM((width, 3 * hidden), bf16),
            pltpu.VMEM((2 * hidden, width), bf16),
            pltpu.SemaphoreType.DMA((dp,)),
        ),
        name="assemble",
        mib=24,
    )(targets, *[x for _, x in held], *other)

    block = (2 * hidden, lane)
    delta, slot_probs, turned, mine, theirs = call(
        delta_kernel,
        (
            sds((all_rows, 2 * hidden), bf16),
            sds((all_rows, lane), bf16),
            sds((2 * hidden, width), bf16),
            sds((ny, *block), bf16),
            sds((ny, *block), bf16),
        ),
        [vmem, hbm, hbm, hbm],
        (near,) * 4 + (hbm,),
        (all_rows * width * hidden * 10, 12 * slot_rows * width),
        scratch=(
            pltpu.VMEM((2 * hidden, all_rows), bf16),
            pltpu.VMEM((all_rows, width), bf16),
            pltpu.VMEM((width, 2 * hidden), bf16),
            pltpu.VMEM((width, hidden), bf16),
            pltpu.VMEM((all_rows, width), bf16),
            pltpu.VMEM((ny, *block), bf16),
            pltpu.SemaphoreType.DMA((ny // 2,)),
            pltpu.SemaphoreType.DMA((weight_chunks + 2,)),
        ),
        name="delta",
        mib=24,
    )(arrived, gate_up, down, turned)
    got = across(theirs)
    returned = call(
        slot_grad_kernel,
        (sds((slot_rows, width + half + lane), bf16),),
        [near] * 3,
        (hbm,),
        (all_rows * width * hidden * 4, 12 * slot_rows * width),
        scratch=(
            pltpu.VMEM((slot_rows, width + half + lane), bf16),
            pltpu.SemaphoreType.DMA((3,)),
        ),
        name="slot_grad",
        mib=24,
    )(delta, slot_probs, turned)[0]
    sums = call(
        pair_sum_kernel,
        (sds(block, bf16),) * ny,
        [near, vmem],
        (hbm,) * ny,
        (width * hidden * 2, 12 * width * hidden),
        scratch=(pltpu.VMEM((ny, *block), bf16), pltpu.SemaphoreType.DMA((ny,))),
        name="pair_sum",
    )(mine, got)
    returned, *sums = lax.optimization_barrier((returned, *sums))
    back = exchange(returned)
    far_first = sorted(range(1, ny), key=lambda d: -min(d, ny - d))
    terms = [sums[0]] + [along_y(sums[d], d) for d in far_first]
    gate_grad, up_grad = call(
        finish_weights_kernel,
        (sds((width // dp, hidden), f32),) * 2,
        [vmem] * (1 + ny),
        (vmem, vmem),
        (width * hidden * 2, 4 * width * hidden),
        name="finish_weights",
    )(decay, *terms)
    token_grad, prob_grad = call(
        finish_tokens_kernel,
        (sds((count, width), bf16), sds((2, count), bf16)),
        [vmem] * 4,
        (vmem, vmem),
        (count * slot_rows * width * 4, 6 * slot_rows * width),
        name="finish_tokens",
        mib=16,
    )(targets, place_left, place_right, back)
    return token_grad, prob_grad.T, gate_grad[None], up_grad[None]


def solution(mesh):
    placed = (
        P(("dp", "expert"), None),
        P(("dp", "expert"), None),
        P(("dp", "expert"), None),
        P(("dp", "expert"), None),
        P("expert", "dp", None),
        P("expert", "dp", None),
        P("expert", None, "dp"),
        P("expert", "dp", None),
        P("expert", "dp", None),
        P("expert", None, "dp"),
    )
    return jax.shard_map(
        per_device,
        mesh=mesh,
        in_specs=placed,
        out_specs=(
            P(("dp", "expert"), None),
            P(("dp", "expert"), None),
            P("expert", "dp", None),
            P("expert", "dp", None),
        ),
        check_vma=False,
    )
```

```python
import functools

import jax
import jax.numpy as jnp
from jax import lax
from jax.experimental import pallas as pl
from jax.experimental.pallas import tpu as pltpu
from jax.sharding import PartitionSpec as P

decay_rate = 24.0
main_slots = 8
tail_slots = 4
lane = 128
large = 56
weight_chunks = 4
f32 = jnp.float32
bf16 = jnp.bfloat16
vmem = pl.BlockSpec(memory_space=pltpu.VMEM)
near = pl.BlockSpec(memory_space=pltpu.VMEM)
hbm = pl.BlockSpec(memory_space=pltpu.HBM)
pins = {id(near): pltpu.VMEM, id(hbm): pltpu.HBM}


def iota(shape, dim):
    return lax.broadcasted_iota(jnp.int32, shape, dim)


def position():
    me = lax.axis_index("dp")
    return lax.shift_right_logical(me, 1), lax.bitwise_and(me, 1)


def dot(a, b, dims=((1,), (0,))):
    return lax.dot_general(a, b, (dims, ((), ())), preferred_element_type=f32)


def call(kernel, out_shape, in_specs, out_specs, cost, scratch=(), name=None, mib=12):
    flops, moved = cost

    def run(*args):
        pinned = [
            pltpu.with_memory_space_constraint(x, pins[id(spec)]) if id(spec) in pins else x
            for x, spec in zip(args, in_specs)
        ]
        return kernel_call(*pinned)

    if isinstance(out_specs, tuple):
        out_shape = tuple(
            pins[id(spec)](s.shape, s.dtype) if id(spec) in pins else s
            for s, spec in zip(out_shape, out_specs)
        )
    kernel_call = pl.pallas_call(
        kernel,
        out_shape=out_shape,
        in_specs=in_specs,
        out_specs=out_specs,
        scratch_shapes=scratch,
        compiler_params=pltpu.CompilerParams(vmem_limit_bytes=mib * 1024 * 1024),
        cost_estimate=pl.CostEstimate(flops=flops, bytes_accessed=moved, transcendentals=0),
        name=name,
    )
    return run


def place_kernel(
    ids_hbm, probs_hbm, tokens_hbm, grads_hbm, out_hbm, target_hbm, ids_ref, probs_ref, tokens, grads, out, target, sems
):
    count, width = tokens.shape
    half = width // 2
    slot_rows = out.shape[0]
    experts = slot_rows // main_slots
    parts = ((ids_hbm, ids_ref), (probs_hbm, probs_ref), (tokens_hbm, tokens), (grads_hbm, grads))
    loads = [pltpu.make_async_copy(x, y, sems.at[k]) for k, (x, y) in enumerate(parts)]
    for load in loads:
        load.start()
    loads[0].wait()
    loads[1].wait()
    ids = [ids_ref[k : k + 1, :] for k in range(2)]
    named = [(iota((experts, count), 0) == ids[k]).astype(f32) for k in range(2)]
    before = (iota((count, count), 0) < iota((count, count), 1)).astype(bf16)
    earlier = dot((named[0] + named[1]).astype(bf16), before)
    row = iota((slot_rows, count), 0)
    main_hit, tail_hit, targets = [], [], []
    for k in range(2):
        slot = jnp.sum(earlier * named[k], axis=0, keepdims=True).astype(jnp.int32)
        main = jnp.where(slot < main_slots, ids[k] * main_slots + slot, -100)
        tail = jnp.where(slot < main_slots, -100, ids[k] * main_slots + slot - main_slots)
        targets += [main, tail]
        main_hit.append(row == main)
        tail_hit.append((row == tail, row == tail + tail_slots))
    probs = [probs_ref[k : k + 1, :].astype(f32) for k in range(2)]
    target[...] = jnp.concatenate([t.astype(f32) for t in targets] + probs + probs, axis=0)
    stores = [pltpu.make_async_copy(target, target_hbm, sems.at[4])]
    stores[0].start()

    def placing(hit, scale):
        return (jnp.where(hit[0], scale[0], 0.0) + jnp.where(hit[1], scale[1], 0.0)).astype(bf16)

    def store(start, size):
        span = (slice(None), pl.ds(start, size))
        sem = sems.at[4 + len(stores)]
        stores.append(pltpu.make_async_copy(out.at[span], out_hbm.at[span], sem))
        stores[-1].start()

    for at, (source, scale) in enumerate(((tokens, (1.0, 1.0)), (grads, probs))):
        base = at * (width + half)
        main = placing(main_hit, scale)
        tail = jnp.concatenate(
            [placing([tail_hit[k][side] for k in range(2)], scale) for side in range(2)], axis=1
        )
        loads[2 + at].wait()
        out[:, base : base + width] = dot(main, source[...]).astype(bf16)
        store(base, width)
        halves = jnp.concatenate([source[:, :half], source[:, half:]], axis=0)
        out[:, base + width : base + width + half] = dot(tail, halves).astype(bf16)
        store(base + width, half)
    for copy in stores:
        copy.wait()


def kept(pattern_ref):
    groups = pattern_ref.shape[0]
    rows = groups * 4
    spread = (iota((rows, groups), 0) // 4 == iota((rows, groups), 1)).astype(bf16)
    p = dot(spread, pattern_ref[...].astype(f32).astype(bf16))
    j = iota(p.shape, 0) % 4
    one = (p == 0.0) | (p == 3.0) | (p == 4.0)
    two = (p == 1.0) | (p == 3.0) | (p == 5.0)
    three = (p == 2.0) | (p >= 4.0)
    keep = ((j == 0) & (p <= 2.0)) | ((j == 1) & one) | ((j == 2) & two) | ((j == 3) & three)
    return keep


def mask_kernel(
    gate_ref, up_ref, down_ref, gate_mask_ref, up_mask_ref, down_mask_ref, out_ref, decay_ref
):
    hidden = gate_ref.shape[1]
    for at, (weight, mask) in enumerate(((gate_ref, gate_mask_ref), (up_ref, up_mask_ref))):
        span = slice(at * hidden, (at + 1) * hidden)
        keep, dense = kept(mask), weight[...].astype(f32)
        out_ref[:, span] = jnp.where(keep, dense, 0.0).astype(bf16)
        decay_ref[:, span] = jnp.where(keep, 0.0, decay_rate * dense)
    masked = jnp.where(kept(down_mask_ref), down_ref[...].astype(f32), 0.0)
    out_ref[:, 2 * hidden :] = masked.T.astype(bf16)


def tail_sides(rows):
    wide = rows * main_slots // tail_slots
    r = iota((rows, wide), 0)
    low = r // tail_slots * main_slots + r % tail_slots
    c = iota((rows, wide), 1)
    return (c == low).astype(bf16), (c == low + tail_slots).astype(bf16)


def tail_sides_t(rows):
    wide = rows * main_slots // tail_slots
    r = iota((wide, rows), 1)
    low = r // tail_slots * main_slots + r % tail_slots
    c = iota((wide, rows), 0)
    return (c == low).astype(bf16), (c == low + tail_slots).astype(bf16)


def assemble_kernel(order, target_ref, *refs):
    pieces = 2 * len(order)
    piece_refs = refs[:pieces]
    weight_hbm, down_hbm, turned_hbm, left_ref, right_ref, weight, turned, sems = refs[pieces:]
    depth = piece_refs[0].shape[0]
    y, core = position()
    copies = []
    for k in range(pieces):
        origin = lax.rem(y + (len(order) - order[k % len(order)]), len(order))
        offset = (2 * origin + (core if k < len(order) else 1 - core)) * depth
        to = weight.at[pl.ds(pl.multiple_of(offset, depth), depth)]
        copies.append(pltpu.make_async_copy(piece_refs[k], to, sems.at[k]))
        copies[-1].start()
    count = target_ref.shape[1]
    slot_rows = left_ref.shape[1] // 2
    row = iota((slot_rows, count), 0).astype(f32)
    main0, tail0, main1, tail1 = [target_ref[k : k + 1, :] for k in range(4)]
    main = ((row == main0) | (row == main1)).astype(f32).T.astype(bf16)
    low = ((row == tail0) | (row == tail1)).astype(f32).T.astype(bf16)
    high = ((row == tail0 + tail_slots) | (row == tail1 + tail_slots)).astype(f32).T.astype(bf16)
    left_ref[:, :slot_rows] = main
    left_ref[:, slot_rows:] = low
    right_ref[:, :slot_rows] = main
    right_ref[:, slot_rows:] = high
    for copy in copies:
        copy.wait()
    gate_up = turned.shape[0]
    stores = [
        pltpu.make_async_copy(weight.at[:, pl.ds(0, gate_up)], weight_hbm, sems.at[0]),
        pltpu.make_async_copy(weight.at[:, pl.ds(gate_up, gate_up // 2)], down_hbm, sems.at[1]),
        pltpu.make_async_copy(turned, turned_hbm, sems.at[2]),
    ]
    stores[0].start()
    stores[1].start()
    for at in range(0, turned.shape[1], 2 * lane):
        turned[:, at : at + 2 * lane] = weight[at : at + 2 * lane, :gate_up].T
    stores[2].start()
    for store in stores:
        store.wait()


def weight_grads(delta_t_ref, rows_ref, out, own, after):
    steps = out.shape[0]
    y, core = position()
    side = (core if own else 1 - core) * lane

    def columns(d):
        at = lax.rem(y + d, steps) * 2 * lane + side
        return rows_ref[:, pl.ds(pl.multiple_of(at, lane), lane)]

    for d in range(0, steps, 2):
        part = dot(delta_t_ref[...], jnp.concatenate([columns(d), columns(d + 1)], axis=1))
        out[d] = part[:, :lane].astype(bf16)
        out[d + 1] = part[:, lane:].astype(bf16)
        after(d)


def delta_kernel(
    x_ref,
    weight_hbm,
    down_hbm,
    turned_hbm,
    delta_ref,
    prob_ref,
    turned,
    mine_ref,
    other_hbm,
    delta_t_ref,
    rows,
    weight,
    down,
    cotan,
    other,
    sems,
    load_sems,
):
    width, hidden = down.shape
    half = width // 2
    depth = width // weight_chunks
    spans = [slice(k * depth, (k + 1) * depth) for k in range(weight_chunks)]
    loads = [
        pltpu.make_async_copy(weight_hbm.at[span], weight.at[span], load_sems.at[k])
        for k, span in enumerate(spans)
    ]
    loads.append(pltpu.make_async_copy(down_hbm, down, load_sems.at[weight_chunks]))
    loads.append(pltpu.make_async_copy(turned_hbm, turned, load_sems.at[weight_chunks + 1]))
    for load in loads:
        load.start()
    main_rows = x_ref.shape[0]
    tail_rows = main_rows * tail_slots // main_slots
    low, high = tail_sides(tail_rows)
    for at, target in enumerate((rows, cotan)):
        base = at * (width + half)
        target[:main_rows, :] = x_ref[:, base : base + width]
        halves = x_ref[:, base + width : base + width + half]
        target[main_rows:, :half] = dot(low, halves).astype(bf16)
        target[main_rows:, half:] = dot(high, halves).astype(bf16)
    pre = 0.0
    for load, span in zip(loads, spans):
        load.wait()
        pre = pre + dot(rows[:, span], weight[span, :])
    loads[-2].wait()
    grad = dot(cotan[...], down[...])
    gate_pre, up_pre = pre[:, :hidden], pre[:, hidden:]
    sig = jax.nn.sigmoid(gate_pre)
    silu = gate_pre * sig
    act = (silu * up_pre).astype(bf16)
    prob = jnp.sum(act.astype(f32) * grad, axis=1, keepdims=True)
    prob_ref[...] = jnp.broadcast_to(prob, prob_ref.shape).astype(bf16)
    gate_delta = (grad * up_pre * sig * (1.0 + gate_pre * (1.0 - sig))).astype(bf16)
    up_delta = (grad * silu).astype(bf16)
    delta_ref[:, :hidden] = gate_delta
    delta_ref[:, hidden:] = up_delta
    delta_t_ref[:hidden, :] = gate_delta.T
    delta_t_ref[hidden:, :] = up_delta.T
    stores = []

    def after(d):
        span = pl.ds(d, 2)
        stores.append(pltpu.make_async_copy(other.at[span], other_hbm.at[span], sems.at[d // 2]))
        stores[-1].start()

    weight_grads(delta_t_ref, rows, other, False, after)
    weight_grads(delta_t_ref, rows, mine_ref, True, lambda d: None)
    for copy in stores + loads[-1:]:
        copy.wait()


def slot_grad_kernel(delta_ref, prob_ref, turned_ref, out_hbm, out, sems):
    width = turned_ref.shape[1]
    half = width // 2
    main_rows = out.shape[0]
    tail_rows = delta_ref.shape[0] - main_rows
    stores = []

    def store(start, size):
        span = (slice(None), pl.ds(start, size))
        sem = sems.at[len(stores)]
        stores.append(pltpu.make_async_copy(out.at[span], out_hbm.at[span], sem))
        stores[-1].start()

    low_t, high_t = tail_sides_t(tail_rows)
    tails = []
    for at in range(2):
        span = slice(at * half, (at + 1) * half)
        back = dot(delta_ref[...], turned_ref[:, span]).astype(bf16)
        out[:, span] = back[:main_rows]
        store(at * half, half)
        tails.append(back[main_rows:])
    tail = dot(low_t, tails[0]) + dot(high_t, tails[1])
    out[:, width : width + half] = tail.astype(bf16)
    at_lane = iota((main_rows, lane), 1)
    late = dot(low_t, prob_ref[main_rows:, :])
    probs = jnp.where(at_lane == 1, late, prob_ref[:main_rows, :].astype(f32))
    out[:, width + half :] = probs.astype(bf16)
    store(width, half + lane)
    for copy in stores:
        copy.wait()


def pair_sum_kernel(mine_ref, got_ref, *refs):
    steps = mine_ref.shape[0]
    outs, sums, sems = refs[:steps], refs[steps], refs[steps + 1]
    stores = []
    for d, out in enumerate(outs):
        sums[d] = (mine_ref[d].astype(f32) + got_ref[d].astype(f32)).astype(bf16)
        stores.append(pltpu.make_async_copy(sums.at[d], out, sems.at[d]))
        stores[-1].start()
    for copy in stores:
        copy.wait()


def finish_weights_kernel(decay_ref, *refs):
    gate_out, up_out = refs[-2:]
    hidden = gate_out.shape[1]
    total = refs[0][...].astype(f32)
    for ref in refs[1:-2]:
        total = total + ref[...].astype(f32)
    total = total.T + decay_ref[...]
    gate_out[...] = total[:, :hidden]
    up_out[...] = total[:, hidden:]


def finish_tokens_kernel(target_ref, left_ref, right_ref, back_ref, grad_ref, prob_ref):
    width = grad_ref.shape[1]
    half = width // 2
    slot_rows = back_ref.shape[0]
    tail = back_ref[:, width : width + half]
    for at, place in enumerate((left_ref, right_ref)):
        span = slice(at * half, (at + 1) * half)
        stacked = jnp.concatenate([back_ref[:, span], tail], axis=0)
        grad_ref[:, span] = dot(place[...], stacked).astype(bf16)
    returned = back_ref[:, width + half :].astype(f32)
    row = iota((slot_rows, target_ref.shape[1]), 0).astype(f32)
    for k in range(2):
        main, late = target_ref[2 * k : 2 * k + 1, :], target_ref[2 * k + 1 : 2 * k + 2, :]
        picked = jnp.where(row == main, returned[:, 0:1], 0.0)
        picked = picked + jnp.where(row == late, returned[:, 1:2], 0.0)
        total = jnp.sum(picked, axis=0, keepdims=True)
        prob_ref[k : k + 1, :] = (total / target_ref[4 + k : 5 + k, :]).astype(bf16)


def per_device(
    tokens,
    out_grad,
    expert_ids,
    route_probs,
    gate_weight,
    up_weight,
    down_weight,
    gate_mask,
    up_mask,
    down_mask,
):
    count, width = tokens.shape
    half = width // 2
    hidden = gate_weight.shape[2]
    experts = lax.axis_size("expert")
    dp = lax.axis_size("dp")
    ny = dp // 2
    slot_rows = experts * main_slots
    all_rows = experts * (main_slots + tail_slots)
    sds = jax.ShapeDtypeStruct
    ids, probs = expert_ids.T, route_probs.T

    sent, targets = call(
        place_kernel,
        (sds((slot_rows, 3 * width), bf16), sds((8, count), f32)),
        [hbm] * 4,
        (hbm, hbm),
        (slot_rows * count * width * 10, 5 * slot_rows * width * 2),
        scratch=(
            pltpu.VMEM((2, count), jnp.int32),
            pltpu.VMEM((2, count), bf16),
            pltpu.VMEM((count, width), bf16),
            pltpu.VMEM((count, width), bf16),
            pltpu.VMEM((slot_rows, 3 * width), bf16),
            pltpu.VMEM((8, count), f32),
            pltpu.SemaphoreType.DMA((9,)),
        ),
        name="place",
        mib=large,
    )(ids, probs, tokens, out_grad)

    def exchange(x):
        blocks = x.reshape(experts, main_slots, x.shape[1])
        moved = lax.all_to_all(blocks, "expert", split_axis=0, concat_axis=0, tiled=True)
        return moved.reshape(x.shape)

    arrived = exchange(sent)

    piece, decay = call(
        mask_kernel,
        (sds((width // dp, 3 * hidden), bf16), sds((width // dp, 2 * hidden), f32)),
        [vmem] * 6,
        (vmem, vmem),
        (width * hidden * 100, 6 * width // dp * hidden),
        name="mask",
        mib=large,
    )(gate_weight[0], up_weight[0], down_weight[0], gate_mask[0], up_mask[0], down_mask[0])

    def along_y(x, d):
        moves = [(2 * a + c, 2 * ((a + d) % ny) + c) for a in range(ny) for c in range(2)]
        return lax.ppermute(x, "dp", moves)

    def across(x):
        return lax.ppermute(x, "dp", [(i, i ^ 1) for i in range(dp)])

    forward, backward = [piece], [piece]
    for _ in range(ny // 2):
        forward.append(along_y(forward[-1], 1))
        backward.append(along_y(backward[-1], ny - 1))
    held = [(0, piece)] + [(d, forward[d]) for d in range(1, ny // 2 + 1)]
    held += [(ny - d, backward[d]) for d in range(1, ny // 2)]
    other = [across(x) for _, x in held]
    gate_up, down, turned, place_left, place_right = call(
        functools.partial(assemble_kernel, [d for d, _ in held]),
        (
            sds((width, 2 * hidden), bf16),
            sds((width, hidden), bf16),
            sds((2 * hidden, width), bf16),
        )
        + (sds((count, 2 * slot_rows), bf16),) * 2,
        [vmem] + [hbm] * dp,
        (hbm, hbm, hbm, vmem, vmem),
        (count * slot_rows * 10, 6 * width * hidden),
        scratch=(
            pltpu.VMEM((width, 3 * hidden), bf16),
            pltpu.VMEM((2 * hidden, width), bf16),
            pltpu.SemaphoreType.DMA((dp,)),
        ),
        name="assemble",
        mib=24,
    )(targets, *[x for _, x in held], *other)

    block = (2 * hidden, lane)
    delta, slot_probs, turned, mine, theirs = call(
        delta_kernel,
        (
            sds((all_rows, 2 * hidden), bf16),
            sds((all_rows, lane), bf16),
            sds((2 * hidden, width), bf16),
            sds((ny, *block), bf16),
            sds((ny, *block), bf16),
        ),
        [vmem, hbm, hbm, hbm],
        (near,) * 4 + (hbm,),
        (all_rows * width * hidden * 10, 12 * slot_rows * width),
        scratch=(
            pltpu.VMEM((2 * hidden, all_rows), bf16),
            pltpu.VMEM((all_rows, width), bf16),
            pltpu.VMEM((width, 2 * hidden), bf16),
            pltpu.VMEM((width, hidden), bf16),
            pltpu.VMEM((all_rows, width), bf16),
            pltpu.VMEM((ny, *block), bf16),
            pltpu.SemaphoreType.DMA((ny // 2,)),
            pltpu.SemaphoreType.DMA((weight_chunks + 2,)),
        ),
        name="delta",
        mib=24,
    )(arrived, gate_up, down, turned)
    got = across(theirs)
    returned = call(
        slot_grad_kernel,
        (sds((slot_rows, width + half + lane), bf16),),
        [near] * 3,
        (hbm,),
        (all_rows * width * hidden * 4, 12 * slot_rows * width),
        scratch=(
            pltpu.VMEM((slot_rows, width + half + lane), bf16),
            pltpu.SemaphoreType.DMA((3,)),
        ),
        name="slot_grad",
        mib=24,
    )(delta, slot_probs, turned)[0]
    sums = call(
        pair_sum_kernel,
        (sds(block, bf16),) * ny,
        [near, vmem],
        (hbm,) * ny,
        (width * hidden * 2, 12 * width * hidden),
        scratch=(pltpu.VMEM((ny, *block), bf16), pltpu.SemaphoreType.DMA((ny,))),
        name="pair_sum",
    )(mine, got)
    returned, *sums = lax.optimization_barrier((returned, *sums))
    back = exchange(returned)
    far_first = sorted(range(1, ny), key=lambda d: -min(d, ny - d))
    terms = [sums[0]] + [along_y(sums[d], d) for d in far_first]
    token_grad, prob_grad = call(
        finish_tokens_kernel,
        (sds((count, width), bf16), sds((2, count), bf16)),
        [vmem] * 4,
        (vmem, vmem),
        (count * slot_rows * width * 4, 6 * slot_rows * width),
        name="finish_tokens",
        mib=16,
    )(targets, place_left, place_right, back)
    decay, prob_grad = lax.optimization_barrier((decay, prob_grad))
    gate_grad, up_grad = call(
        finish_weights_kernel,
        (sds((width // dp, hidden), f32),) * 2,
        [vmem] * (1 + ny),
        (vmem, vmem),
        (width * hidden * 2, 4 * width * hidden),
        name="finish_weights",
    )(decay, *terms)
    return token_grad, prob_grad.T, gate_grad[None], up_grad[None]


def solution(mesh):
    placed = (
        P(("dp", "expert"), None),
        P(("dp", "expert"), None),
        P(("dp", "expert"), None),
        P(("dp", "expert"), None),
        P("expert", "dp", None),
        P("expert", "dp", None),
        P("expert", None, "dp"),
        P("expert", "dp", None),
        P("expert", "dp", None),
        P("expert", None, "dp"),
    )
    return jax.shard_map(
        per_device,
        mesh=mesh,
        in_specs=placed,
        out_specs=(
            P(("dp", "expert"), None),
            P(("dp", "expert"), None),
            P("expert", "dp", None),
            P("expert", "dp", None),
        ),
        check_vma=False,
    )
```
